32 devices in a mesh: grp: 2 (over y), seg: 2 (over core), inner: 8 (over z, x).
Axes of the slice: x: 2, y: 2, z: 4, core: 2. Of those that a mesh axis runs over, the one named last changes fastest.
Arguments:
- queries: bfloat16 [8192, 8, 128], P(('grp', 'seg', 'inner')), parts along dimension 0, may hold values from -5.5 to 5.5
- keys: bfloat16 [8192, 8, 128], P(('grp', 'seg', 'inner')), parts along dimension 0, may hold values from -6 to 6
- values: bfloat16 [8192, 8, 128], P(('grp', 'seg', 'inner')), parts along dimension 0, may hold values from -6 to 6
- strengths: float32 [8192, 8], P(('grp', 'seg', 'inner')), parts along dimension 0, may hold values from 0.001 to 1.95, as said below
Outputs:
- outputs: bfloat16 [8192, 8, 128], P(('grp', 'seg', 'inner')), parts along dimension 0
The draws below stay inside these ranges and needn't reach their ends.
There are 2 independent parts, one for each index of `grp`. The reference program is written for one: setup_inputs(seed, part) draws one part's arguments, and reference() takes and returns one part's arrays. A program takes and returns all parts, laid end to end along the dimension named above; each array names one. Nothing has to cross between parts.
Inputs may be any that keep to these rules, and one draw needn't show every extreme that they name: Positive reflection strengths; a head's strengths lie within a factor of three of each other.
All inputs are finite; a program needn't handle non-finite values.
Results may differ from the reference program's by a relative error of at most 0.001.
Values sent between devices are 32-bit elements; how exact they have to be, the bound alone decides.
A program may use at most 512 MiB of HBM per device.

```python
import math
import jax
import jax.numpy as jnp
from jax import lax

HEADS = 8
DK = 128
DV = 128
TOK_DEV = 256
TOKENS = 4096


def shared_signs(key):
    flips = jax.random.bernoulli(jax.random.fold_in(key, 101), 0.5, (HEADS, DK))
    return jnp.where(flips, 1.0, -1.0).astype(jnp.float32)


def draw_keys(key, part):
    k_mask, k_amp, k_sub, k_rest = jax.random.split(jax.random.fold_in(key, 202), 4)
    shards = TOKENS // TOK_DEV
    signs = shared_signs(key)
    mask = jax.random.bernoulli(k_mask, 0.25, (shards, 1, HEADS, DK)).astype(jnp.float32)
    amp = jax.random.uniform(k_amp, (TOKENS, HEADS, 1), jnp.float32, 0.8, 1.2)
    sub_noise = jnp.clip(jax.random.normal(k_sub, (shards, TOK_DEV, HEADS, DK), jnp.float32), -4.0, 4.0)
    rest_noise = jnp.clip(jax.random.normal(k_rest, (TOKENS, HEADS, DK), jnp.float32), -4.0, 4.0)
    local_part = (sub_noise * mask).reshape(TOKENS, HEADS, DK)
    result = amp * 0.8 * signs[None] + local_part + 0.25 * rest_noise
    return result.astype(jnp.bfloat16)


def draw_queries(key, part):
    k_amp, k_noise = jax.random.split(jax.random.fold_in(key, 303), 2)
    signs = shared_signs(key)
    amp = jax.random.uniform(k_amp, (TOKENS, HEADS, 1), jnp.float32, 0.7, 1.3)
    noise = jnp.clip(jax.random.normal(k_noise, (TOKENS, HEADS, DK), jnp.float32), -4.0, 4.0)
    return (amp * signs[None] + noise).astype(jnp.bfloat16)


def draw_strengths(key, part):
    k_pick, k_slow, k_fast, k_token = jax.random.split(key, 4)
    slow = jax.random.bernoulli(k_pick, 0.5, (HEADS,))
    slow_rate = jnp.exp(jax.random.uniform(k_slow, (HEADS,), jnp.float32, math.log(0.004), math.log(0.016)))
    fast_rate = jnp.exp(jax.random.uniform(k_fast, (HEADS,), jnp.float32, math.log(0.3), math.log(1.3)))
    rate = jnp.where(slow, slow_rate, fast_rate)
    factor = jax.random.uniform(k_token, (TOKENS, HEADS), jnp.float32, 0.5, 1.5)
    return (rate[None, :] * factor).astype(jnp.float32)


def block_levels(stream_key, dims, cuts, smallest, high):
    factor_of, own = 1.0, jax.random.fold_in(stream_key, 6)
    for position, parts in cuts:
        steps = jnp.exp(jax.random.uniform(jax.random.fold_in(own, position), (parts,), jnp.float32, smallest / len(cuts), high / len(cuts)))
        factor_of = factor_of * jnp.repeat(steps, dims[position] // parts).reshape([-1 if axis == position else 1 for axis in range(len(dims))])
    return factor_of


def centred(stream_key, shape, scale, bound, cuts=(), held_as=jnp.bfloat16):
    drawn = jax.random.normal(stream_key, shape, jnp.float32) * scale
    if len(cuts) > 0:
        drawn = block_levels(stream_key, shape, cuts, -0.22, 0.18) * drawn
    return jnp.clip(drawn, min=-bound, max=bound).astype(held_as)


def setup_inputs(seed: int = 0, part: int = 0) -> dict:
    streams_of = jax.random.split(jax.random.key(seed), 5)
    own_keys = jax.random.split(jax.random.fold_in(streams_of[4], part), 5)
    queries = draw_queries(jax.random.fold_in(jax.random.fold_in(streams_of[4], part), 71), part)
    keys = draw_keys(jax.random.fold_in(jax.random.fold_in(streams_of[4], part), 71), part)
    values = centred(own_keys[2], (TOKENS, HEADS, DV), 1.0, 6.0, ((0, 16),))
    strengths = draw_strengths(jax.random.fold_in(jax.random.fold_in(streams_of[4], part), 71), part)
    return dict(queries=queries, keys=keys, values=values, strengths=strengths)


def unit_rows(field):
    field = field.astype(jnp.float32)
    return field * lax.rsqrt(lax.optimization_barrier(jnp.sum(field * field, axis=-1, keepdims=True)) + 1e-06)

def block_terms(queries, keys, values, strengths):
    hp = lax.Precision.HIGHEST
    query_h = jnp.transpose(unit_rows(queries), (1, 0, 2))
    key_h = jnp.transpose(unit_rows(keys), (1, 0, 2))
    value_h = jnp.transpose(values.astype(jnp.float32), (1, 0, 2))
    beta_h = jnp.transpose(strengths.astype(jnp.float32), (1, 0))[:, :, None]
    rows = key_h.shape[1]
    gram = jnp.einsum('hid,hjd->hij', key_h, key_h, precision=hp)
    lower = jnp.tril(gram, -1) * beta_h
    system = jnp.eye(rows, dtype=jnp.float32)[None] + lower
    right = jnp.concatenate([beta_h * value_h, beta_h * key_h], axis=-1)
    solved = jax.scipy.linalg.solve_triangular(system, right, lower=True, unit_diagonal=True)
    width_v = value_h.shape[2]
    ubar = solved[..., :width_v]
    wmat = solved[..., width_v:]
    scores = jnp.tril(jnp.einsum('hid,hjd->hij', query_h, key_h, precision=hp))
    local_out = jnp.einsum('hij,hjv->hiv', scores, ubar, precision=hp)
    query_fix = query_h - jnp.einsum('hij,hjd->hid', scores, wmat, precision=hp)
    width_k = key_h.shape[2]
    trans = jnp.eye(width_k, dtype=jnp.float32)[None] - jnp.einsum('hcd,hce->hde', wmat, key_h, precision=hp)
    offset = jnp.einsum('hcv,hcd->hvd', ubar, key_h, precision=hp)
    return (trans, offset, local_out, query_fix)

def reference(queries, keys, values, strengths):
    hp = lax.Precision.HIGHEST
    block = min(128, TOK_DEV)
    count = TOKENS // block
    qs = queries.reshape(count, block, HEADS, DK)
    ks = keys.reshape(count, block, HEADS, DK)
    vs = values.reshape(count, block, HEADS, DV)
    bs = strengths.reshape(count, block, HEADS)

    def advance(state, pieces):
        trans, offset, local_out, query_fix = block_terms(pieces[0], pieces[1], pieces[2], pieces[3])
        result = local_out + jnp.einsum('hcd,hvd->hcv', query_fix, state, precision=hp)
        state = jnp.einsum('hvd,hde->hve', state, trans, precision=hp) + offset
        return (state, jnp.transpose(result, (1, 0, 2)))
    start = jnp.zeros((HEADS, DV, DK), jnp.float32)
    final, blocks = lax.scan(advance, start, (qs, ks, vs, bs))
    return blocks.reshape(TOKENS, HEADS, DV).astype(jnp.bfloat16)
```

```python
import functools

import jax
import jax.numpy as jnp
from jax import lax
from jax.experimental import pallas as pl
from jax.experimental.pallas import tpu as pltpu
from jax.sharding import PartitionSpec as P

F32 = jnp.float32
BF16 = jnp.bfloat16
NN = (((1,), (0,)), ((), ()))
NT = (((1,), (1,)), ((), ()))
TN = (((0,), (0,)), ((), ()))
VMEM_LIMIT = 48 * 1024 * 1024


def dot(a, b, dims=NN):
    return lax.dot_general(a, b, dims, preferred_element_type=F32)


def split(a):
    high = a.astype(BF16)
    return high, (a - high.astype(F32)).astype(BF16)


def dot2(a, b, dims=NN):
    return dot(a[0], b, dims) + dot(a[1], b, dims)


def dot3(a, b, dims=NN):
    return dot(a[0], b[0], dims) + (dot(a[0], b[1], dims) + dot(a[1], b[0], dims))


def inverse_unit_norm(field):
    return lax.rsqrt(jnp.sum(field * field, axis=-1, keepdims=True) + 1e-06)


def head_terms(q, k, v, beta):
    rows, width = k.shape
    wide_v = v.shape[1]
    rk = inverse_unit_norm(k.astype(F32))
    qf = q.astype(F32)
    rq = inverse_unit_norm(qf)
    lane = lax.broadcasted_iota(jnp.int32, (rows, 128), 1)
    packed = jnp.where(lane == 0, rk, jnp.where(lane == 1, beta, 0.0)).T
    rk_row = packed[0:1]
    beta_row = packed[1:2]
    row = lax.broadcasted_iota(jnp.int32, (rows, rows), 0)
    col = lax.broadcasted_iota(jnp.int32, (rows, rows), 1)
    lower = jnp.where(row > col, dot(k, k, NT) * (beta * rk) * rk_row, 0.0)
    scores = split(jnp.where(row >= col, dot(q, k, NT) * rq * rk_row, 0.0))
    low_h, low_l = split(lower)
    inv = jnp.where(row == col, 1.0, 0.0) - jnp.where((row >> 1) == (col >> 1), lower, 0.0)
    bit = 1
    zero = jnp.zeros((), BF16)
    while (1 << bit) < rows:
        mask = (row >> bit) == ((col >> bit) ^ 1)
        cut = (jnp.where(mask, low_h, zero), jnp.where(mask, low_l, zero))
        halves = split(inv)
        inv = inv - dot3(halves, split(dot3(cut, halves)))
        bit += 1
    inv_v = inv * beta_row
    ubar = dot2(split(inv_v), v)
    wmat = dot2(split(inv_v * rk_row), k)
    both = jnp.concatenate([ubar, wmat], axis=1)
    mixed = dot3(scores, split(both))
    local = mixed[:, :wide_v]
    fix = qf * rq - mixed[:, wide_v:]
    maps = dot2(split(both * rk), k, TN)
    eye = jnp.where(
        lax.broadcasted_iota(jnp.int32, (width, width), 0)
        == lax.broadcasted_iota(jnp.int32, (width, width), 1),
        1.0,
        0.0,
    )
    return eye - maps[wide_v:], maps[:wide_v], local, fix


def local_kernel(q_ref, k_ref, v_ref, s_ref, th_ref, tl_ref, o_ref, lo_ref, qh_ref, ql_ref, wide, qs, ks, vs):
    heads = q_ref.shape[1]
    for source, target in ((k_ref, ks), (v_ref, vs), (q_ref, qs)):
        wide[...] = source[...].astype(F32)
        for h in range(heads):
            target[h] = wide[:, h, :].astype(BF16)
    strengths = s_ref[...]
    lane = lax.broadcasted_iota(jnp.int32, strengths.shape, 1)

    def pair(step, unused):
        for half in range(2):
            h = step * 2 + half
            beta = jnp.sum(jnp.where(lane == h, strengths, 0.0), axis=1, keepdims=True)
            trans, offset, local, fix = head_terms(qs[h], ks[h], vs[h], beta)
            th_ref[h], tl_ref[h] = split(trans)
            o_ref[h] = offset
            lo_ref[h] = local
            qh_ref[h], ql_ref[h] = split(fix)
        return unused

    lax.fori_loop(0, heads // 2, pair, 0)


def chain_kernel(segs, inners, th_ref, tl_ref, o_ref, in_ref, landed, leaving, send_sem, recv_sem):
    heads = o_ref.shape[0]
    total = segs * inners
    me = lax.axis_index("seg") * inners + lax.axis_index("inner")

    def place(index):
        index = lax.rem(index + total, total)
        return {"seg": index // inners, "inner": lax.rem(index, inners)}

    barrier = pltpu.get_barrier_semaphore()
    for step in (-1, 1):
        pl.semaphore_signal(barrier, inc=1, device_id=place(me + step), device_id_type=pl.DeviceIdType.MESH)
    pl.semaphore_wait(barrier, 2)

    def hop(h):
        return pltpu.make_async_remote_copy(
            src_ref=leaving.at[h],
            dst_ref=landed.at[h],
            send_sem=send_sem.at[h],
            recv_sem=recv_sem.at[h],
            device_id=place(me + 1),
            device_id_type=pl.DeviceIdType.MESH,
        )

    for h in range(heads):

        @pl.when(me > 0)
        def _():
            hop(h).wait_recv()
            state = landed[h]
            in_ref[h] = state

            @pl.when(me < total - 1)
            def _():
                leaving[h] = o_ref[h] + dot3(split(state), (th_ref[h], tl_ref[h]))

        @pl.when(me == 0)
        def _():
            in_ref[h] = jnp.zeros_like(in_ref[h])
            leaving[h] = o_ref[h]

        @pl.when(me < total - 1)
        def _():
            hop(h).start()

    @pl.when(me < total - 1)
    def _():
        for h in range(heads):
            hop(h).wait_send()


def emit_kernel(in_ref, lo_ref, qh_ref, ql_ref, out_ref, wide):
    heads = in_ref.shape[0]
    for h in range(heads):
        wide[:, h, :] = lo_ref[h] + dot3((qh_ref[h], ql_ref[h]), split(in_ref[h]), NT)
    out_ref[...] = wide[...].astype(out_ref.dtype)


def body(segs, inners, queries, keys, values, strengths):
    rows, heads, width = queries.shape
    wide_v = values.shape[2]
    vm = pl.BlockSpec(memory_space=pltpu.VMEM)
    shape = jax.ShapeDtypeStruct
    params = pltpu.CompilerParams(vmem_limit_bytes=VMEM_LIMIT)
    th, tl, off, local, qh, ql = pl.pallas_call(
        local_kernel,
        out_shape=[
            shape((heads, width, width), BF16),
            shape((heads, width, width), BF16),
            shape((heads, wide_v, width), F32),
            shape((heads, rows, wide_v), F32),
            shape((heads, rows, width), BF16),
            shape((heads, rows, width), BF16),
        ],
        in_specs=[vm] * 4,
        out_specs=[vm] * 6,
        scratch_shapes=[
            pltpu.VMEM((rows, heads, width), F32),
            pltpu.VMEM((heads, rows, width), BF16),
            pltpu.VMEM((heads, rows, width), BF16),
            pltpu.VMEM((heads, rows, wide_v), BF16),
        ],
        compiler_params=params,
        name="local_terms",
    )(queries, keys, values, strengths)
    entering = pl.pallas_call(
        functools.partial(chain_kernel, segs, inners),
        out_shape=shape((heads, wide_v, width), F32),
        in_specs=[vm] * 3,
        out_specs=vm,
        scratch_shapes=[
            pltpu.VMEM((heads, wide_v, width), F32),
            pltpu.VMEM((heads, wide_v, width), F32),
            pltpu.SemaphoreType.DMA((heads,)),
            pltpu.SemaphoreType.DMA((heads,)),
        ],
        compiler_params=pltpu.CompilerParams(
            collective_id=0, has_side_effects=True, vmem_limit_bytes=VMEM_LIMIT
        ),
        name="state_chain",
    )(th, tl, off)
    return pl.pallas_call(
        emit_kernel,
        out_shape=shape((rows, heads, wide_v), BF16),
        in_specs=[vm] * 4,
        out_specs=vm,
        scratch_shapes=[pltpu.VMEM((rows, heads, wide_v), F32)],
        compiler_params=params,
        name="emit",
    )(entering, local, qh, ql)


def solution(mesh):
    split_rows = ("grp", "seg", "inner")
    placed = (
        P(split_rows, None, None),
        P(split_rows, None, None),
        P(split_rows, None, None),
        P(split_rows, None),
    )
    return jax.shard_map(
        functools.partial(body, mesh.shape["seg"], mesh.shape["inner"]),
        mesh=mesh,
        in_specs=placed,
        out_specs=P(split_rows, None, None),
        check_vma=False,
    )
```

```python
import functools

import jax
import jax.numpy as jnp
from jax import lax
from jax.experimental import pallas as pl
from jax.experimental.pallas import tpu as pltpu
from jax.sharding import PartitionSpec as P

F32 = jnp.float32
BF16 = jnp.bfloat16
NN = (((1,), (0,)), ((), ()))
NT = (((1,), (1,)), ((), ()))
TN = (((0,), (0,)), ((), ()))
GROUP = 2
VMEM_LIMIT = 48 * 1024 * 1024


def dot(a, b, dims=NN):
    return lax.dot_general(a, b, dims, preferred_element_type=F32)


def split(a):
    high = a.astype(BF16)
    return high, (a - high.astype(F32)).astype(BF16)


def dot2(a, b, dims=NN):
    return dot(a[0], b, dims) + dot(a[1], b, dims)


def dot3(a, b, dims=NN):
    (left,), (right,) = dims[0]
    if a[0].shape[left] == 128:
        joined = dot(
            jnp.concatenate([a[0], a[1]], axis=left),
            jnp.concatenate([b[0], b[0]], axis=right),
            dims,
        )
        return joined + dot(a[0], b[1], dims)
    return dot(a[0], b[0], dims) + (dot(a[0], b[1], dims) + dot(a[1], b[0], dims))


def inverse_unit_norm(field):
    return lax.rsqrt(jnp.sum(field * field, axis=-1, keepdims=True) + 1e-06)


def iotas(rows):
    return (
        lax.broadcasted_iota(jnp.int32, (rows, rows), 0),
        lax.broadcasted_iota(jnp.int32, (rows, rows), 1),
    )


def unit_lower_inverses(blocks):
    rows = blocks[0].shape[0]
    row, col = iotas(rows)
    eye = jnp.where(row == col, 1.0, 0.0)
    first = (row >> 1) == (col >> 1)
    inverses = [eye - jnp.where(first, n, 0.0) for n in blocks]
    lowers = [split(n) for n in blocks]
    bit = 1
    while (1 << bit) < rows:
        mask = (row >> bit) == ((col >> bit) ^ 1)
        halves = [split(x) for x in inverses]
        right = [split(dot3(n, x)) for n, x in zip(lowers, halves)]
        whole = [dot3(x, y) for x, y in zip(halves, right)]
        inverses = [x - jnp.where(mask, w, 0.0) for x, w in zip(inverses, whole)]
        bit += 1
    return inverses


def group_terms(group):
    rows, width = group[0][1].shape
    wide_v = group[0][2].shape[1]
    half = rows // 2
    row, col = iotas(rows)
    lane = lax.broadcasted_iota(jnp.int32, (rows, 128), 1)
    lowers, sides, blocks = [], [], []
    for q, k, v, beta in group:
        rk = inverse_unit_norm(k.astype(F32))
        packed = jnp.where(lane == 0, rk, jnp.where(lane == 1, beta, 0.0)).T
        lower = jnp.where(row > col, dot(k, k, NT) * (beta * rk) * packed[0:1], 0.0)
        lowers.append(lower)
        sides.append((rk, packed[0:1], packed[1:2]))
        blocks += [lower[:half, :half], lower[half:, half:]]
    diagonal = unit_lower_inverses(blocks)
    halves = [split(x) for x in diagonal]
    corners = [
        split(dot3(split(n[half:, :half]), halves[2 * i])) for i, n in enumerate(lowers)
    ]
    corners = [dot3(halves[2 * i + 1], c) for i, c in enumerate(corners)]
    zero = jnp.zeros((half, half), F32)
    inverses = [
        jnp.concatenate(
            [
                jnp.concatenate([diagonal[2 * i], zero], axis=1),
                jnp.concatenate([-c, diagonal[2 * i + 1]], axis=1),
            ],
            axis=0,
        )
        for i, c in enumerate(corners)
    ]
    eye = jnp.where(iotas(width)[0] == iotas(width)[1], 1.0, 0.0)
    results = []
    for (q, k, v, beta), (rk, rk_row, beta_row), inv in zip(group, sides, inverses):
        inv_v = inv * beta_row
        ubar = dot2(split(inv_v), v)
        wmat = dot2(split(inv_v * rk_row), k)
        both = jnp.concatenate([ubar, wmat], axis=1)
        maps = dot2(split(both * rk), k, TN)
        results.append((eye - maps[wide_v:], maps[:wide_v], both, rk_row))
    return results


def query_terms(q, k, both, rk_row):
    rows = q.shape[0]
    wide_v = both.shape[1] - k.shape[1]
    row, col = iotas(rows)
    qf = q.astype(F32)
    rq = inverse_unit_norm(qf)
    scores = jnp.where(row >= col, dot(q, k, NT) * rq * rk_row, 0.0)
    mixed = dot3(split(scores), split(both))
    return mixed[:, :wide_v], qf * rq - mixed[:, wide_v:]


def maps_kernel(
    segs, inners, q_ref, k_ref, v_ref, s_ref, in_ref, lo_ref, qh_ref, ql_ref,
    wide, qs, ks, vs, own, earlier, pair, landed, leaving,
    map_send, map_recv, next_send, fan_send, state_recv,
):
    heads = q_ref.shape[1]
    wide_k = own.shape[2]
    total = segs * inners
    me = lax.axis_index("seg") * inners + lax.axis_index("inner")
    odd = lax.rem(me, 2) == 1
    even = lax.rem(me, 2) == 0
    first = me < 2
    last = me >= total - 2

    def place(index):
        index = lax.rem(index + total, total)
        return {"seg": index // inners, "inner": lax.rem(index, inners)}

    barrier = pltpu.get_barrier_semaphore()
    for step in (-2, -1, 1, 2):
        pl.semaphore_signal(barrier, inc=1, device_id=place(me + step), device_id_type=pl.DeviceIdType.MESH)

    def send(source, target, send_sem, recv_sem, h, step):
        return pltpu.make_async_remote_copy(
            src_ref=source.at[h],
            dst_ref=target.at[h],
            send_sem=send_sem.at[h],
            recv_sem=recv_sem.at[h],
            device_id=place(me + step),
            device_id_type=pl.DeviceIdType.MESH,
        )

    def map_hop(h):
        return send(own, earlier, map_send, map_recv, h, 1)

    def next_hop(h):
        return send(leaving, landed, next_send, state_recv, h, 2)

    def fan_hop(h):
        return send(leaving, landed, fan_send, state_recv, h, 1)

    for source, target in ((k_ref, ks), (v_ref, vs), (q_ref, qs)):
        wide[...] = source[...].astype(F32)
        for h in range(heads):
            target[h] = wide[:, h, :].astype(BF16)
    strengths = s_ref[...]
    lane = lax.broadcasted_iota(jnp.int32, strengths.shape, 1)
    pl.semaphore_wait(barrier, 4)

    def local(step, unused):
        places = [step * GROUP + i for i in range(GROUP)]
        group = []
        for h in places:
            beta = jnp.sum(jnp.where(lane == h, strengths, 0.0), axis=1, keepdims=True)
            group.append((qs[h], ks[h], vs[h], beta))
        terms = group_terms(group)
        for h, (trans, offset, both, rk_row) in zip(places, terms):
            own[h, :wide_k, :] = trans
            own[h, wide_k:, :] = offset

        @pl.when(even)
        def _():
            for h in places:
                map_hop(h).start()

        for h, (q, k, v, beta), (trans, offset, both, rk_row) in zip(places, group, terms):
            lo_ref[h], fix = query_terms(q, k, both, rk_row)
            qh_ref[h], ql_ref[h] = split(fix)
        return unused

    lax.fori_loop(0, heads // GROUP, local, 0)

    @pl.when(odd)
    def _():
        def compose(h, unused):
            map_hop(h).wait_recv()
            both = dot3(split(earlier[h]), split(own[h, :wide_k, :]))
            pair[h, :wide_k, :] = both[:wide_k]
            pair[h, wide_k:, :] = both[wide_k:] + own[h, wide_k:, :]
            return unused

        def advance(h, unused):
            @pl.when(first)
            def _():
                landed[h] = jnp.zeros_like(landed[h])

            @pl.when(jnp.logical_not(first))
            def _():
                next_hop(h).wait_recv()

            state = split(landed[h])

            @pl.when(jnp.logical_not(last))
            def _():
                leaving[h] = dot3(state, split(pair[h, :wide_k, :])) + pair[h, wide_k:, :]
                next_hop(h).start()
                fan_hop(h).start()

            in_ref[h] = dot3(state, split(earlier[h, :wide_k, :])) + earlier[h, wide_k:, :]
            return unused

        lax.fori_loop(0, heads, compose, 0)
        lax.fori_loop(0, heads, advance, 0)

        @pl.when(jnp.logical_not(last))
        def _():
            for h in range(heads):
                next_hop(h).wait_send()
                fan_hop(h).wait_send()

    @pl.when(even)
    def _():
        for h in range(heads):
            map_hop(h).wait_send()

        @pl.when(first)
        def _():
            in_ref[...] = jnp.zeros_like(in_ref)

        @pl.when(jnp.logical_not(first))
        def _():
            for h in range(heads):
                fan_hop(h).wait_recv()
            in_ref[...] = landed[...]


def emit_kernel(in_ref, lo_ref, qh_ref, ql_ref, out_ref, wide):
    heads = in_ref.shape[0]
    for h in range(heads):
        wide[:, h, :] = lo_ref[h] + dot3((qh_ref[h], ql_ref[h]), split(in_ref[h]), NT)
    out_ref[...] = wide[...].astype(out_ref.dtype)


def body(segs, inners, queries, keys, values, strengths):
    rows, heads, width = queries.shape
    wide_v = values.shape[2]
    vm = pl.BlockSpec(memory_space=pltpu.VMEM)
    shape = jax.ShapeDtypeStruct
    params = pltpu.CompilerParams(vmem_limit_bytes=VMEM_LIMIT)
    dma = pltpu.SemaphoreType.DMA((heads,))
    maps = pltpu.VMEM((heads, width + wide_v, width), F32)
    states = pltpu.VMEM((heads, wide_v, width), F32)
    entering, local, qh, ql = pl.pallas_call(
        functools.partial(maps_kernel, segs, inners),
        out_shape=[
            shape((heads, wide_v, width), F32),
            shape((heads, rows, wide_v), F32),
            shape((heads, rows, width), BF16),
            shape((heads, rows, width), BF16),
        ],
        in_specs=[vm] * 4,
        out_specs=[vm] * 4,
        scratch_shapes=[
            pltpu.VMEM((rows, heads, width), F32),
            pltpu.VMEM((heads, rows, width), BF16),
            pltpu.VMEM((heads, rows, width), BF16),
            pltpu.VMEM((heads, rows, wide_v), BF16),
            maps, maps, maps, states, states,
            dma, dma, dma, dma, dma,
        ],
        compiler_params=pltpu.CompilerParams(
            collective_id=0, has_side_effects=True, vmem_limit_bytes=VMEM_LIMIT
        ),
        name="maps_and_chain",
    )(queries, keys, values, strengths)
    return pl.pallas_call(
        emit_kernel,
        out_shape=shape((rows, heads, wide_v), BF16),
        in_specs=[vm] * 4,
        out_specs=vm,
        scratch_shapes=[pltpu.VMEM((rows, heads, wide_v), F32)],
        compiler_params=params,
        name="emit",
    )(entering, local, qh, ql)


def solution(mesh):
    split_rows = ("grp", "seg", "inner")
    placed = (
        P(split_rows, None, None),
        P(split_rows, None, None),
        P(split_rows, None, None),
        P(split_rows, None),
    )
    return jax.shard_map(
        functools.partial(body, mesh.shape["seg"], mesh.shape["inner"]),
        mesh=mesh,
        in_specs=placed,
        out_specs=P(split_rows, None, None),
        check_vma=False,
    )
```

```python
import functools

import jax
import jax.numpy as jnp
from jax import lax
from jax.experimental import pallas as pl
from jax.experimental.pallas import tpu as pltpu
from jax.sharding import PartitionSpec as P

F32 = jnp.float32
BF16 = jnp.bfloat16
NN = (((1,), (0,)), ((), ()))
NT = (((1,), (1,)), ((), ()))
TN = (((0,), (0,)), ((), ()))
GROUP = 2
VMEM_LIMIT = 48 * 1024 * 1024


def dot(a, b, dims=NN):
    return lax.dot_general(a, b, dims, preferred_element_type=F32)


def split(a):
    high = a.astype(BF16)
    return high, (a - high.astype(F32)).astype(BF16)


def dot2(a, b, dims=NN):
    return dot(a[0], b, dims) + dot(a[1], b, dims)


def dot3(a, b, dims=NN):
    (left,), (right,) = dims[0]
    if a[0].shape[left] == 128:
        joined = dot(
            jnp.concatenate([a[0], a[1]], axis=left),
            jnp.concatenate([b[0], b[0]], axis=right),
            dims,
        )
        return joined + dot(a[0], b[1], dims)
    return dot(a[0], b[0], dims) + (dot(a[0], b[1], dims) + dot(a[1], b[0], dims))


def inverse_unit_norm(field):
    return lax.rsqrt(jnp.sum(field * field, axis=-1, keepdims=True) + 1e-06)


def iotas(rows):
    return (
        lax.broadcasted_iota(jnp.int32, (rows, rows), 0),
        lax.broadcasted_iota(jnp.int32, (rows, rows), 1),
    )


def unit_lower_inverses(blocks):
    rows = blocks[0].shape[0]
    row, col = iotas(rows)
    eye = jnp.where(row == col, 1.0, 0.0)
    first = (row >> 1) == (col >> 1)
    inverses = [eye - jnp.where(first, n, 0.0) for n in blocks]
    lowers = [split(n) for n in blocks]
    bit = 1
    while (1 << bit) < rows:
        mask = (row >> bit) == ((col >> bit) ^ 1)
        halves = [split(x) for x in inverses]
        right = [split(dot3(n, x)) for n, x in zip(lowers, halves)]
        whole = [dot3(x, y) for x, y in zip(halves, right)]
        inverses = [x - jnp.where(mask, w, 0.0) for x, w in zip(inverses, whole)]
        bit += 1
    return inverses


def group_terms(group):
    rows, width = group[0][1].shape
    wide_v = group[0][2].shape[1]
    half = rows // 2
    row, col = iotas(rows)
    lane = lax.broadcasted_iota(jnp.int32, (rows, 128), 1)
    lowers, sides, blocks = [], [], []
    for q, k, v, beta in group:
        rk = inverse_unit_norm(k.astype(F32))
        packed = jnp.where(lane == 0, rk, jnp.where(lane == 1, beta, 0.0)).T
        lower = jnp.where(row > col, dot(k, k, NT) * (beta * rk) * packed[0:1], 0.0)
        lowers.append(lower)
        sides.append((rk, packed[0:1], packed[1:2]))
        blocks += [lower[:half, :half], lower[half:, half:]]
    diagonal = unit_lower_inverses(blocks)
    halves = [split(x) for x in diagonal]
    corners = [
        split(dot3(split(n[half:, :half]), halves[2 * i])) for i, n in enumerate(lowers)
    ]
    corners = [dot3(halves[2 * i + 1], c) for i, c in enumerate(corners)]
    zero = jnp.zeros((half, half), F32)
    inverses = [
        jnp.concatenate(
            [
                jnp.concatenate([diagonal[2 * i], zero], axis=1),
                jnp.concatenate([-c, diagonal[2 * i + 1]], axis=1),
            ],
            axis=0,
        )
        for i, c in enumerate(corners)
    ]
    eye = jnp.where(iotas(width)[0] == iotas(width)[1], 1.0, 0.0)
    results = []
    for (q, k, v, beta), (rk, rk_row, beta_row), inv in zip(group, sides, inverses):
        inv_v = inv * beta_row
        ubar = dot2(split(inv_v), v)
        wmat = dot2(split(inv_v * rk_row), k)
        both = jnp.concatenate([ubar, wmat], axis=1)
        maps = dot2(split(both * rk), k, TN)
        results.append((eye - maps[wide_v:], maps[:wide_v], both, rk_row))
    return results


def query_terms(q, k, both, rk_row):
    rows = q.shape[0]
    wide_v = both.shape[1] - k.shape[1]
    row, col = iotas(rows)
    qf = q.astype(F32)
    rq = inverse_unit_norm(qf)
    scores = jnp.where(row >= col, dot(q, k, NT) * rq * rk_row, 0.0)
    mixed = dot3(split(scores), split(both))
    return mixed[:, :wide_v], qf * rq - mixed[:, wide_v:]


def maps_kernel(
    segs, inners, q_ref, k_ref, v_ref, s_ref, in_ref, lo_ref, qh_ref, ql_ref,
    wide, qs, ks, vs, solved, scale, own, earlier, pair_h, pair_l, pair_o, landed, leaving,
    map_send, map_recv, next_send, fan_send, state_recv,
):
    heads = q_ref.shape[1]
    wide_k = own.shape[2]
    total = segs * inners
    me = lax.axis_index("seg") * inners + lax.axis_index("inner")
    odd = lax.rem(me, 2) == 1
    even = lax.rem(me, 2) == 0
    first = me < 2
    last = me >= total - 2

    def place(index):
        index = lax.rem(index + total, total)
        return {"seg": index // inners, "inner": lax.rem(index, inners)}

    barrier = pltpu.get_barrier_semaphore()
    for step in (-2, -1, 1, 2):
        pl.semaphore_signal(barrier, inc=1, device_id=place(me + step), device_id_type=pl.DeviceIdType.MESH)

    def send(source, target, send_sem, recv_sem, h, step):
        return pltpu.make_async_remote_copy(
            src_ref=source.at[h],
            dst_ref=target.at[h],
            send_sem=send_sem.at[h],
            recv_sem=recv_sem.at[h],
            device_id=place(me + step),
            device_id_type=pl.DeviceIdType.MESH,
        )

    def map_hop(h):
        return send(own, earlier, map_send, map_recv, h, 1)

    def next_hop(h):
        return send(leaving, landed, next_send, state_recv, h, 2)

    def fan_hop(h):
        return send(landed, landed, fan_send, state_recv, h, -1)

    for source, target in ((k_ref, ks), (v_ref, vs), (q_ref, qs)):
        wide[...] = source[...].astype(F32)
        for h in range(heads):
            target[h] = wide[:, h, :].astype(BF16)
    strengths = s_ref[...]
    lane = lax.broadcasted_iota(jnp.int32, strengths.shape, 1)
    pl.semaphore_wait(barrier, 4)

    def local(step, unused):
        places = [step * GROUP + i for i in range(GROUP)]
        group = []
        for h in places:
            beta = jnp.sum(jnp.where(lane == h, strengths, 0.0), axis=1, keepdims=True)
            group.append((qs[h], ks[h], vs[h], beta))
        terms = group_terms(group)
        for h, (trans, offset, both, rk_row) in zip(places, terms):
            own[h, :wide_k, :] = trans
            own[h, wide_k:, :] = offset
            solved[h] = both
            scale[h] = jnp.broadcast_to(rk_row, scale.shape[1:])

        @pl.when(even)
        def _():
            for h in places:
                map_hop(h).start()

        return unused

    lax.fori_loop(0, heads // GROUP, local, 0)

    def query_side(step, unused):
        for i in range(GROUP):
            h = step * GROUP + i
            lo_ref[h], fix = query_terms(qs[h], ks[h], solved[h], scale[h, 0:1, :])
            qh_ref[h], ql_ref[h] = split(fix)
        return unused

    early = jnp.logical_and(odd, me < total // 2)

    @pl.when(jnp.logical_not(early))
    def _():
        lax.fori_loop(0, heads // GROUP, query_side, 0)

    def enter(h):
        in_ref[h] = dot3(split(landed[h]), split(earlier[h, :wide_k, :])) + earlier[h, wide_k:, :]

    @pl.when(odd)
    def _():
        for h in range(heads):
            map_hop(h).wait_recv()
            later = split(own[h, :wide_k, :])

            @pl.when(first)
            def _():
                offset = dot3(split(earlier[h, wide_k:, :]), later)
                leaving[h] = offset + own[h, wide_k:, :]
                next_hop(h).start()

            @pl.when(jnp.logical_not(first))
            def _():
                both = dot3(split(earlier[h]), later)
                pair_h[h], pair_l[h] = split(both[:wide_k])
                pair_o[h] = both[wide_k:] + own[h, wide_k:, :]

        def advance(h, unused):
            next_hop(h).wait_recv()

            @pl.when(jnp.logical_not(last))
            def _():
                leaving[h] = dot3(split(landed[h]), (pair_h[h], pair_l[h])) + pair_o[h]
                next_hop(h).start()

            fan_hop(h).start()

            @pl.when(last)
            def _():
                enter(h)

            return unused

        @pl.when(first)
        def _():
            for h in range(heads):
                in_ref[h] = earlier[h, wide_k:, :]

        @pl.when(jnp.logical_not(first))
        def _():
            lax.fori_loop(0, heads, advance, 0)

        @pl.when(jnp.logical_not(jnp.logical_or(first, last)))
        def _():
            for h in range(heads):
                enter(h)

    @pl.when(early)
    def _():
        lax.fori_loop(0, heads // GROUP, query_side, 0)

    @pl.when(jnp.logical_and(odd, jnp.logical_not(last)))
    def _():
        for h in range(heads):
            next_hop(h).wait_send()

    @pl.when(jnp.logical_and(odd, jnp.logical_not(first)))
    def _():
        for h in range(heads):
            fan_hop(h).wait_send()

    @pl.when(even)
    def _():
        for h in range(heads):
            map_hop(h).wait_send()

        @pl.when(first)
        def _():
            in_ref[...] = jnp.zeros_like(in_ref)

        @pl.when(jnp.logical_not(first))
        def _():
            for h in range(heads):
                fan_hop(h).wait_recv()
            in_ref[...] = landed[...]


def emit_kernel(in_ref, lo_ref, qh_ref, ql_ref, out_ref, wide):
    heads = in_ref.shape[0]
    for h in range(heads):
        wide[:, h, :] = lo_ref[h] + dot3((qh_ref[h], ql_ref[h]), split(in_ref[h]), NT)
    out_ref[...] = wide[...].astype(out_ref.dtype)


def body(segs, inners, queries, keys, values, strengths):
    rows, heads, width = queries.shape
    wide_v = values.shape[2]
    vm = pl.BlockSpec(memory_space=pltpu.VMEM)
    shape = jax.ShapeDtypeStruct
    params = pltpu.CompilerParams(vmem_limit_bytes=VMEM_LIMIT)
    dma = pltpu.SemaphoreType.DMA((heads,))
    maps = pltpu.VMEM((heads, width + wide_v, width), F32)
    halves = pltpu.VMEM((heads, width, width), BF16)
    states = pltpu.VMEM((heads, wide_v, width), F32)
    entering, local, qh, ql = pl.pallas_call(
        functools.partial(maps_kernel, segs, inners),
        out_shape=[
            shape((heads, wide_v, width), F32),
            shape((heads, rows, wide_v), F32),
            shape((heads, rows, width), BF16),
            shape((heads, rows, width), BF16),
        ],
        in_specs=[vm] * 4,
        out_specs=[vm] * 4,
        scratch_shapes=[
            pltpu.VMEM((rows, heads, width), F32),
            pltpu.VMEM((heads, rows, width), BF16),
            pltpu.VMEM((heads, rows, width), BF16),
            pltpu.VMEM((heads, rows, wide_v), BF16),
            pltpu.VMEM((heads, rows, wide_v + width), F32),
            pltpu.VMEM((heads, 8, rows), F32),
            maps, maps, halves, halves, states, states, states,
            dma, dma, dma, dma, dma,
        ],
        compiler_params=pltpu.CompilerParams(
            collective_id=0, has_side_effects=True, vmem_limit_bytes=VMEM_LIMIT
        ),
        name="maps_and_chain",
    )(queries, keys, values, strengths)
    return pl.pallas_call(
        emit_kernel,
        out_shape=shape((rows, heads, wide_v), BF16),
        in_specs=[vm] * 4,
        out_specs=vm,
        scratch_shapes=[pltpu.VMEM((rows, heads, wide_v), F32)],
        compiler_params=params,
        name="emit",
    )(entering, local, qh, ql)


def solution(mesh):
    split_rows = ("grp", "seg", "inner")
    placed = (
        P(split_rows, None, None),
        P(split_rows, None, None),
        P(split_rows, None, None),
        P(split_rows, None),
    )
    return jax.shard_map(
        functools.partial(body, mesh.shape["seg"], mesh.shape["inner"]),
        mesh=mesh,
        in_specs=placed,
        out_specs=P(split_rows, None, None),
        check_vma=False,
    )
```

```python
import functools

import jax
import jax.numpy as jnp
from jax import lax
from jax.experimental import pallas as pl
from jax.experimental.pallas import tpu as pltpu
from jax.sharding import PartitionSpec as P

F32 = jnp.float32
BF16 = jnp.bfloat16
NN = (((1,), (0,)), ((), ()))
NT = (((1,), (1,)), ((), ()))
TN = (((0,), (0,)), ((), ()))
GROUP = 4
VMEM_LIMIT = 48 * 1024 * 1024


def dot(a, b, dims=NN):
    return lax.dot_general(a, b, dims, preferred_element_type=F32)


def split(a):
    high = a.astype(BF16)
    return high, (a - high.astype(F32)).astype(BF16)


def dot2(a, b, dims=NN):
    return dot(a[0], b, dims) + dot(a[1], b, dims)


def dot3(a, b, dims=NN):
    (left,), (right,) = dims[0]
    if a[0].shape[left] == 128:
        joined = dot(
            jnp.concatenate([a[0], a[1]], axis=left),
            jnp.concatenate([b[0], b[0]], axis=right),
            dims,
        )
        return joined + dot(a[0], b[1], dims)
    return dot(a[0], b[0], dims) + (dot(a[0], b[1], dims) + dot(a[1], b[0], dims))


def inverse_unit_norm(field):
    return lax.rsqrt(jnp.sum(field * field, axis=-1, keepdims=True) + 1e-06)


def iotas(rows):
    return (
        lax.broadcasted_iota(jnp.int32, (rows, rows), 0),
        lax.broadcasted_iota(jnp.int32, (rows, rows), 1),
    )


def unit_lower_inverses(blocks):
    rows = blocks[0].shape[0]
    row, col = iotas(rows)
    eye = jnp.where(row == col, 1.0, 0.0)
    first = (row >> 1) == (col >> 1)
    inverses = [eye - jnp.where(first, n, 0.0) for n in blocks]
    lowers = [split(n) for n in blocks]
    bit = 1
    while (1 << bit) < rows:
        mask = (row >> bit) == ((col >> bit) ^ 1)
        halves = [split(x) for x in inverses]
        right = [split(dot3(n, x)) for n, x in zip(lowers, halves)]
        whole = [dot3(x, y) for x, y in zip(halves, right)]
        inverses = [x - jnp.where(mask, w, 0.0) for x, w in zip(inverses, whole)]
        bit += 1
    return inverses


def group_terms(group):
    rows, width = group[0][1].shape
    wide_v = group[0][2].shape[1]
    half = rows // 2
    row, col = iotas(rows)
    lane = lax.broadcasted_iota(jnp.int32, (rows, 128), 1)
    lowers, sides, blocks = [], [], []
    for q, k, v, beta in group:
        rk = inverse_unit_norm(k.astype(F32))
        packed = jnp.where(lane == 0, rk, jnp.where(lane == 1, beta, 0.0)).T
        lower = jnp.where(row > col, dot(k, k, NT) * (beta * rk) * packed[0:1], 0.0)
        lowers.append(lower)
        sides.append((rk, packed[0:1], packed[1:2]))
        blocks += [lower[:half, :half], lower[half:, half:]]
    diagonal = unit_lower_inverses(blocks)
    halves = [split(x) for x in diagonal]
    corners = [
        split(dot3(split(n[half:, :half]), halves[2 * i])) for i, n in enumerate(lowers)
    ]
    corners = [dot3(halves[2 * i + 1], c) for i, c in enumerate(corners)]
    zero = jnp.zeros((half, half), F32)
    inverses = [
        jnp.concatenate(
            [
                jnp.concatenate([diagonal[2 * i], zero], axis=1),
                jnp.concatenate([-c, diagonal[2 * i + 1]], axis=1),
            ],
            axis=0,
        )
        for i, c in enumerate(corners)
    ]
    eye = jnp.where(iotas(width)[0] == iotas(width)[1], 1.0, 0.0)
    results = []
    for (q, k, v, beta), (rk, rk_row, beta_row), inv in zip(group, sides, inverses):
        inv_v = inv * beta_row
        ubar = dot2(split(inv_v), v)
        wmat = dot2(split(inv_v * rk_row), k)
        both = jnp.concatenate([ubar, wmat], axis=1)
        maps = dot2(split(both * rk), k, TN)
        results.append((eye - maps[wide_v:], maps[:wide_v], both, rk_row))
    return results


def query_terms(q, k, both, rk_row):
    rows = q.shape[0]
    wide_v = both.shape[1] - k.shape[1]
    row, col = iotas(rows)
    qf = q.astype(F32)
    rq = inverse_unit_norm(qf)
    scores = jnp.where(row >= col, dot(q, k, NT) * rq * rk_row, 0.0)
    mixed = dot3(split(scores), split(both))
    return mixed[:, :wide_v], qf * rq - mixed[:, wide_v:]


def maps_kernel(
    segs, inners, q_ref, k_ref, v_ref, s_ref, in_ref, lo_ref, qh_ref, ql_ref,
    wide, qs, ks, vs, solved, scale, own, earlier, pair_h, pair_l, pair_o, landed, leaving,
    map_send, map_recv, next_send, fan_send, state_recv,
):
    heads = q_ref.shape[1]
    wide_k = own.shape[2]
    total = segs * inners
    me = lax.axis_index("seg") * inners + lax.axis_index("inner")
    odd = lax.rem(me, 2) == 1
    even = lax.rem(me, 2) == 0
    first = me < 2
    last = me >= total - 2

    def place(index):
        index = lax.rem(index + total, total)
        return {"seg": index // inners, "inner": lax.rem(index, inners)}

    barrier = pltpu.get_barrier_semaphore()
    for step in (-2, -1, 1, 2):
        pl.semaphore_signal(barrier, inc=1, device_id=place(me + step), device_id_type=pl.DeviceIdType.MESH)

    def send(source, target, send_sem, recv_sem, h, step):
        return pltpu.make_async_remote_copy(
            src_ref=source.at[h],
            dst_ref=target.at[h],
            send_sem=send_sem.at[h],
            recv_sem=recv_sem.at[h],
            device_id=place(me + step),
            device_id_type=pl.DeviceIdType.MESH,
        )

    def map_hop(h):
        return send(own, earlier, map_send, map_recv, h, 1)

    def next_hop(h):
        return send(leaving, landed, next_send, state_recv, h, 2)

    def fan_hop(h):
        return send(landed, landed, fan_send, state_recv, h, -1)

    for source, target in ((k_ref, ks), (v_ref, vs), (q_ref, qs)):
        wide[...] = source[...].astype(F32)
        for h in range(heads):
            target[h] = wide[:, h, :].astype(BF16)
    strengths = s_ref[...]
    lane = lax.broadcasted_iota(jnp.int32, strengths.shape, 1)
    pl.semaphore_wait(barrier, 4)

    def local(step, unused):
        places = [step * GROUP + i for i in range(GROUP)]
        group = []
        for h in places:
            beta = jnp.sum(jnp.where(lane == h, strengths, 0.0), axis=1, keepdims=True)
            group.append((qs[h], ks[h], vs[h], beta))
        terms = group_terms(group)
        for h, (trans, offset, both, rk_row) in zip(places, terms):
            own[h, :wide_k, :] = trans
            own[h, wide_k:, :] = offset
            solved[h] = both
            scale[h] = jnp.broadcast_to(rk_row, scale.shape[1:])

        @pl.when(even)
        def _():
            for h in places:
                map_hop(h).start()

        return unused

    lax.fori_loop(0, heads // GROUP, local, 0)

    def query_side(step, unused):
        for i in range(GROUP):
            h = step * GROUP + i
            lo_ref[h], fix = query_terms(qs[h], ks[h], solved[h], scale[h, 0:1, :])
            qh_ref[h], ql_ref[h] = split(fix)
        return unused

    early = jnp.logical_and(odd, me < total // 2)

    @pl.when(jnp.logical_not(early))
    def _():
        lax.fori_loop(0, heads // GROUP, query_side, 0)

    def enter(h):
        in_ref[h] = dot3(split(landed[h]), split(earlier[h, :wide_k, :])) + earlier[h, wide_k:, :]

    @pl.when(odd)
    def _():
        for h in range(heads):
            map_hop(h).wait_recv()
            later = split(own[h, :wide_k, :])

            @pl.when(first)
            def _():
                offset = dot3(split(earlier[h, wide_k:, :]), later)
                leaving[h] = offset + own[h, wide_k:, :]
                next_hop(h).start()

            @pl.when(jnp.logical_not(first))
            def _():
                both = dot3(split(earlier[h]), later)
                pair_h[h], pair_l[h] = split(both[:wide_k])
                pair_o[h] = both[wide_k:] + own[h, wide_k:, :]

        def advance(h, unused):
            next_hop(h).wait_recv()

            @pl.when(jnp.logical_not(last))
            def _():
                leaving[h] = dot3(split(landed[h]), (pair_h[h], pair_l[h])) + pair_o[h]
                next_hop(h).start()

            fan_hop(h).start()

            @pl.when(last)
            def _():
                enter(h)

            return unused

        @pl.when(first)
        def _():
            for h in range(heads):
                in_ref[h] = earlier[h, wide_k:, :]

        @pl.when(jnp.logical_not(first))
        def _():
            lax.fori_loop(0, heads, advance, 0)

        @pl.when(jnp.logical_not(jnp.logical_or(first, last)))
        def _():
            for h in range(heads):
                enter(h)

    @pl.when(early)
    def _():
        lax.fori_loop(0, heads // GROUP, query_side, 0)

    @pl.when(jnp.logical_and(odd, jnp.logical_not(last)))
    def _():
        for h in range(heads):
            next_hop(h).wait_send()

    @pl.when(jnp.logical_and(odd, jnp.logical_not(first)))
    def _():
        for h in range(heads):
            fan_hop(h).wait_send()

    @pl.when(even)
    def _():
        for h in range(heads):
            map_hop(h).wait_send()

        @pl.when(first)
        def _():
            in_ref[...] = jnp.zeros_like(in_ref)

        @pl.when(jnp.logical_not(first))
        def _():
            for h in range(heads):
                fan_hop(h).wait_recv()
            in_ref[...] = landed[...]


def emit_kernel(in_ref, lo_ref, qh_ref, ql_ref, out_ref, wide):
    heads = in_ref.shape[0]
    for h in range(heads):
        wide[:, h, :] = lo_ref[h] + dot3((qh_ref[h], ql_ref[h]), split(in_ref[h]), NT)
    out_ref[...] = wide[...].astype(out_ref.dtype)


def body(segs, inners, queries, keys, values, strengths):
    rows, heads, width = queries.shape
    wide_v = values.shape[2]
    vm = pl.BlockSpec(memory_space=pltpu.VMEM)
    shape = jax.ShapeDtypeStruct
    params = pltpu.CompilerParams(vmem_limit_bytes=VMEM_LIMIT)
    dma = pltpu.SemaphoreType.DMA((heads,))
    maps = pltpu.VMEM((heads, width + wide_v, width), F32)
    halves = pltpu.VMEM((heads, width, width), BF16)
    states = pltpu.VMEM((heads, wide_v, width), F32)
    entering, local, qh, ql = pl.pallas_call(
        functools.partial(maps_kernel, segs, inners),
        out_shape=[
            shape((heads, wide_v, width), F32),
            shape((heads, rows, wide_v), F32),
            shape((heads, rows, width), BF16),
            shape((heads, rows, width), BF16),
        ],
        in_specs=[vm] * 4,
        out_specs=[vm] * 4,
        scratch_shapes=[
            pltpu.VMEM((rows, heads, width), F32),
            pltpu.VMEM((heads, rows, width), BF16),
            pltpu.VMEM((heads, rows, width), BF16),
            pltpu.VMEM((heads, rows, wide_v), BF16),
            pltpu.VMEM((heads, rows, wide_v + width), F32),
            pltpu.VMEM((heads, 8, rows), F32),
            maps, maps, halves, halves, states, states, states,
            dma, dma, dma, dma, dma,
        ],
        compiler_params=pltpu.CompilerParams(
            collective_id=0, has_side_effects=True, vmem_limit_bytes=VMEM_LIMIT
        ),
        name="maps_and_chain",
    )(queries, keys, values, strengths)
    return pl.pallas_call(
        emit_kernel,
        out_shape=shape((rows, heads, wide_v), BF16),
        in_specs=[vm] * 4,
        out_specs=vm,
        scratch_shapes=[pltpu.VMEM((rows, heads, wide_v), F32)],
        compiler_params=params,
        name="emit",
    )(entering, local, qh, ql)


def solution(mesh):
    split_rows = ("grp", "seg", "inner")
    placed = (
        P(split_rows, None, None),
        P(split_rows, None, None),
        P(split_rows, None, None),
        P(split_rows, None),
    )
    return jax.shard_map(
        functools.partial(body, mesh.shape["seg"], mesh.shape["inner"]),
        mesh=mesh,
        in_specs=placed,
        out_specs=P(split_rows, None, None),
        check_vma=False,
    )
```

```python
import functools

import jax
import jax.numpy as jnp
from jax import lax
from jax.experimental import pallas as pl
from jax.experimental.pallas import tpu as pltpu
from jax.sharding import PartitionSpec as P

F32 = jnp.float32
BF16 = jnp.bfloat16
NN = (((1,), (0,)), ((), ()))
NT = (((1,), (1,)), ((), ()))
TN = (((0,), (0,)), ((), ()))
GROUP = 2
VMEM_LIMIT = 48 * 1024 * 1024


def dot(a, b, dims=NN):
    return lax.dot_general(a, b, dims, preferred_element_type=F32)


def split(a):
    high = a.astype(BF16)
    return high, (a - high.astype(F32)).astype(BF16)


def dot2(a, b, dims=NN):
    return dot(a[0], b, dims) + dot(a[1], b, dims)


def dot3(a, b, dims=NN):
    (left,), (right,) = dims[0]
    if a[0].shape[left] == 128:
        joined = dot(
            jnp.concatenate([a[0], a[1]], axis=left),
            jnp.concatenate([b[0], b[0]], axis=right),
            dims,
        )
        return joined + dot(a[0], b[1], dims)
    return dot(a[0], b[0], dims) + (dot(a[0], b[1], dims) + dot(a[1], b[0], dims))


def inverse_unit_norm(field):
    return lax.rsqrt(jnp.sum(field * field, axis=-1, keepdims=True) + 1e-06)


def iotas(rows):
    return (
        lax.broadcasted_iota(jnp.int32, (rows, rows), 0),
        lax.broadcasted_iota(jnp.int32, (rows, rows), 1),
    )


def unit_lower_inverses(blocks):
    rows = blocks[0].shape[0]
    row, col = iotas(rows)
    eye = jnp.where(row == col, 1.0, 0.0)
    first = (row >> 1) == (col >> 1)
    inverses = [eye - jnp.where(first, n, 0.0) for n in blocks]
    lowers = [split(n) for n in blocks]
    bit = 1
    while (1 << bit) < rows:
        mask = (row >> bit) == ((col >> bit) ^ 1)
        halves = [split(x) for x in inverses]
        right = [split(dot3(n, x)) for n, x in zip(lowers, halves)]
        whole = [dot3(x, y) for x, y in zip(halves, right)]
        inverses = [x - jnp.where(mask, w, 0.0) for x, w in zip(inverses, whole)]
        bit += 1
    return inverses


def group_terms(group):
    rows, width = group[0][1].shape
    wide_v = group[0][2].shape[1]
    half = rows // 2
    row, col = iotas(rows)
    lane = lax.broadcasted_iota(jnp.int32, (rows, 128), 1)
    lowers, sides, blocks = [], [], []
    for q, k, v, beta in group:
        rk = inverse_unit_norm(k.astype(F32))
        packed = jnp.where(lane == 0, rk, jnp.where(lane == 1, beta, 0.0)).T
        lower = jnp.where(row > col, dot(k, k, NT) * (beta * rk) * packed[0:1], 0.0)
        lowers.append(lower)
        sides.append((rk, packed[0:1], packed[1:2]))
        blocks += [lower[:half, :half], lower[half:, half:]]
    diagonal = unit_lower_inverses(blocks)
    halves = [split(x) for x in diagonal]
    corners = [
        split(dot3(split(n[half:, :half]), halves[2 * i])) for i, n in enumerate(lowers)
    ]
    corners = [dot3(halves[2 * i + 1], c) for i, c in enumerate(corners)]
    zero = jnp.zeros((half, half), F32)
    inverses = [
        jnp.concatenate(
            [
                jnp.concatenate([diagonal[2 * i], zero], axis=1),
                jnp.concatenate([-c, diagonal[2 * i + 1]], axis=1),
            ],
            axis=0,
        )
        for i, c in enumerate(corners)
    ]
    eye = jnp.where(iotas(width)[0] == iotas(width)[1], 1.0, 0.0)
    results = []
    for (q, k, v, beta), (rk, rk_row, beta_row), inv in zip(group, sides, inverses):
        inv_v = inv * beta_row
        ubar = dot2(split(inv_v), v)
        wmat = dot2(split(inv_v * rk_row), k)
        both = jnp.concatenate([ubar, wmat], axis=1)
        maps = dot2(split(both * rk), k, TN)
        results.append((eye - maps[wide_v:], maps[:wide_v], both, rk_row))
    return results


def query_terms(q, k, both, rk_row):
    rows = q.shape[0]
    wide_v = both.shape[1] - k.shape[1]
    row, col = iotas(rows)
    qf = q.astype(F32)
    rq = inverse_unit_norm(qf)
    scores = jnp.where(row >= col, dot(q, k, NT) * rq * rk_row, 0.0)
    mixed = dot3(split(scores), split(both))
    return mixed[:, :wide_v], qf * rq - mixed[:, wide_v:]


def maps_kernel(
    segs, inners, q_ref, k_ref, v_ref, s_ref, in_ref, lo_ref, qh_ref, ql_ref,
    wide, qs, ks, vs, solved, scale, own, earlier, pair_h, pair_l, pair_o, landed, leaving,
    map_send, map_recv, next_send, fan_send, state_recv,
):
    heads = q_ref.shape[1]
    wide_k = own.shape[2]
    total = segs * inners
    me = lax.axis_index("seg") * inners + lax.axis_index("inner")
    odd = lax.rem(me, 2) == 1
    even = lax.rem(me, 2) == 0
    first = me < 2
    last = me >= total - 2

    def place(index):
        index = lax.rem(index + total, total)
        return {"seg": index // inners, "inner": lax.rem(index, inners)}

    barrier = pltpu.get_barrier_semaphore()
    for step in (-2, -1, 1, 2):
        pl.semaphore_signal(barrier, inc=1, device_id=place(me + step), device_id_type=pl.DeviceIdType.MESH)

    def send(source, target, send_sem, recv_sem, h, step):
        return pltpu.make_async_remote_copy(
            src_ref=source.at[h],
            dst_ref=target.at[h],
            send_sem=send_sem.at[h],
            recv_sem=recv_sem.at[h],
            device_id=place(me + step),
            device_id_type=pl.DeviceIdType.MESH,
        )

    def map_hop(h):
        return send(own, earlier, map_send, map_recv, h, 1)

    def next_hop(h):
        return send(leaving, landed, next_send, state_recv, h, 2)

    def fan_hop(h):
        return send(landed, landed, fan_send, state_recv, h, -1)

    for source, target in ((k_ref, ks), (v_ref, vs), (q_ref, qs)):
        wide[...] = source[...].astype(F32)
        for h in range(heads):
            target[h] = wide[:, h, :].astype(BF16)
    strengths = s_ref[...]
    lane = lax.broadcasted_iota(jnp.int32, strengths.shape, 1)
    pl.semaphore_wait(barrier, 4)

    def local(step, unused):
        places = [step * GROUP + i for i in range(GROUP)]
        group = []
        for h in places:
            beta = jnp.sum(jnp.where(lane == h, strengths, 0.0), axis=1, keepdims=True)
            group.append((qs[h], ks[h], vs[h], beta))
        terms = group_terms(group)
        for h, (trans, offset, both, rk_row) in zip(places, terms):
            own[h, :wide_k, :] = trans
            own[h, wide_k:, :] = offset
            solved[h] = both
            scale[h] = jnp.broadcast_to(rk_row, scale.shape[1:])

        @pl.when(jnp.logical_and(even, jnp.logical_or(me < total // 2, step < heads // GROUP - 1)))
        def _():
            for h in places:
                map_hop(h).start()

        return unused

    lax.fori_loop(0, heads // GROUP, local, 0)

    def query_side(step, unused):
        for i in range(GROUP):
            h = step * GROUP + i
            lo_ref[h], fix = query_terms(qs[h], ks[h], solved[h], scale[h, 0:1, :])
            qh_ref[h], ql_ref[h] = split(fix)
        return unused

    early = jnp.logical_and(odd, me < total // 2)

    @pl.when(jnp.logical_not(early))
    def _():
        lax.fori_loop(0, heads // GROUP, query_side, 0)

    @pl.when(jnp.logical_and(even, me >= total // 2))
    def _():
        for h in range(heads - GROUP, heads):
            map_hop(h).start()

    def enter(h):
        in_ref[h] = dot3(split(landed[h]), split(earlier[h, :wide_k, :])) + earlier[h, wide_k:, :]

    @pl.when(odd)
    def _():
        def compose(h):
            map_hop(h).wait_recv()
            later = split(own[h, :wide_k, :])

            @pl.when(first)
            def _():
                offset = dot3(split(earlier[h, wide_k:, :]), later)
                leaving[h] = offset + own[h, wide_k:, :]
                next_hop(h).start()

            @pl.when(jnp.logical_not(first))
            def _():
                both = dot3(split(earlier[h]), later)
                pair_h[h], pair_l[h] = split(both[:wide_k])
                pair_o[h] = both[wide_k:] + own[h, wide_k:, :]

        def advance(h, unused):
            next_hop(h).wait_recv()

            @pl.when(jnp.logical_not(last))
            def _():
                leaving[h] = dot3(split(landed[h]), (pair_h[h], pair_l[h])) + pair_o[h]
                next_hop(h).start()

            fan_hop(h).start()

            @pl.when(last)
            def _():
                enter(h)

            return unused

        for low, high in ((0, heads - GROUP), (heads - GROUP, heads)):
            for h in range(low, high):
                compose(h)

            @pl.when(jnp.logical_not(first))
            def _():
                lax.fori_loop(low, high, advance, 0)

        @pl.when(first)
        def _():
            for h in range(heads):
                in_ref[h] = earlier[h, wide_k:, :]

        @pl.when(jnp.logical_not(jnp.logical_or(first, last)))
        def _():
            for h in range(heads):
                enter(h)

    @pl.when(early)
    def _():
        lax.fori_loop(0, heads // GROUP, query_side, 0)

    @pl.when(jnp.logical_and(odd, jnp.logical_not(last)))
    def _():
        for h in range(heads):
            next_hop(h).wait_send()

    @pl.when(jnp.logical_and(odd, jnp.logical_not(first)))
    def _():
        for h in range(heads):
            fan_hop(h).wait_send()

    @pl.when(even)
    def _():
        for h in range(heads):
            map_hop(h).wait_send()

        @pl.when(first)
        def _():
            in_ref[...] = jnp.zeros_like(in_ref)

        @pl.when(jnp.logical_not(first))
        def _():
            for h in range(heads):
                fan_hop(h).wait_recv()
            in_ref[...] = landed[...]


def emit_kernel(in_ref, lo_ref, qh_ref, ql_ref, out_ref, wide):
    heads = in_ref.shape[0]
    for h in range(heads):
        wide[:, h, :] = lo_ref[h] + dot3((qh_ref[h], ql_ref[h]), split(in_ref[h]), NT)
    out_ref[...] = wide[...].astype(out_ref.dtype)


def body(segs, inners, queries, keys, values, strengths):
    rows, heads, width = queries.shape
    wide_v = values.shape[2]
    vm = pl.BlockSpec(memory_space=pltpu.VMEM)
    shape = jax.ShapeDtypeStruct
    params = pltpu.CompilerParams(vmem_limit_bytes=VMEM_LIMIT)
    dma = pltpu.SemaphoreType.DMA((heads,))
    maps = pltpu.VMEM((heads, width + wide_v, width), F32)
    halves = pltpu.VMEM((heads, width, width), BF16)
    states = pltpu.VMEM((heads, wide_v, width), F32)
    entering, local, qh, ql = pl.pallas_call(
        functools.partial(maps_kernel, segs, inners),
        out_shape=[
            shape((heads, wide_v, width), F32),
            shape((heads, rows, wide_v), F32),
            shape((heads, rows, width), BF16),
            shape((heads, rows, width), BF16),
        ],
        in_specs=[vm] * 4,
        out_specs=[vm] * 4,
        scratch_shapes=[
            pltpu.VMEM((rows, heads, width), F32),
            pltpu.VMEM((heads, rows, width), BF16),
            pltpu.VMEM((heads, rows, width), BF16),
            pltpu.VMEM((heads, rows, wide_v), BF16),
            pltpu.VMEM((heads, rows, wide_v + width), F32),
            pltpu.VMEM((heads, 8, rows), F32),
            maps, maps, halves, halves, states, states, states,
            dma, dma, dma, dma, dma,
        ],
        compiler_params=pltpu.CompilerParams(
            collective_id=0, has_side_effects=True, vmem_limit_bytes=VMEM_LIMIT
        ),
        name="maps_and_chain",
    )(queries, keys, values, strengths)
    return pl.pallas_call(
        emit_kernel,
        out_shape=shape((rows, heads, wide_v), BF16),
        in_specs=[vm] * 4,
        out_specs=vm,
        scratch_shapes=[pltpu.VMEM((rows, heads, wide_v), F32)],
        compiler_params=params,
        name="emit",
    )(entering, local, qh, ql)


def solution(mesh):
    split_rows = ("grp", "seg", "inner")
    placed = (
        P(split_rows, None, None),
        P(split_rows, None, None),
        P(split_rows, None, None),
        P(split_rows, None),
    )
    return jax.shard_map(
        functools.partial(body, mesh.shape["seg"], mesh.shape["inner"]),
        mesh=mesh,
        in_specs=placed,
        out_specs=P(split_rows, None, None),
        check_vma=False,
    )
```

```python
import functools

import jax
import jax.numpy as jnp
from jax import lax
from jax.experimental import pallas as pl
from jax.experimental.pallas import tpu as pltpu
from jax.sharding import PartitionSpec as P

F32 = jnp.float32
BF16 = jnp.bfloat16
NN = (((1,), (0,)), ((), ()))
NT = (((1,), (1,)), ((), ()))
TN = (((0,), (0,)), ((), ()))
GROUP = 2
VMEM_LIMIT = 48 * 1024 * 1024


def dot(a, b, dims=NN):
    return lax.dot_general(a, b, dims, preferred_element_type=F32)


def split(a):
    high = a.astype(BF16)
    return high, (a - high.astype(F32)).astype(BF16)


def dot2(a, b, dims=NN):
    return dot(a[0], b, dims) + dot(a[1], b, dims)


def dot3(a, b, dims=NN):
    (left,), (right,) = dims[0]
    if a[0].shape[left] == 128:
        joined = dot(
            jnp.concatenate([a[0], a[1]], axis=left),
            jnp.concatenate([b[0], b[0]], axis=right),
            dims,
        )
        return joined + dot(a[0], b[1], dims)
    return dot(a[0], b[0], dims) + (dot(a[0], b[1], dims) + dot(a[1], b[0], dims))


def inverse_unit_norm(field):
    return lax.rsqrt(jnp.sum(field * field, axis=-1, keepdims=True) + 1e-06)


def iotas(rows):
    return (
        lax.broadcasted_iota(jnp.int32, (rows, rows), 0),
        lax.broadcasted_iota(jnp.int32, (rows, rows), 1),
    )


def unit_lower_inverses(blocks):
    rows = blocks[0].shape[0]
    row, col = iotas(rows)
    eye = jnp.where(row == col, 1.0, 0.0)
    first = (row >> 1) == (col >> 1)
    inverses = [eye - jnp.where(first, n, 0.0) for n in blocks]
    lowers = [split(n) for n in blocks]
    bit = 1
    while (1 << bit) < rows:
        mask = (row >> bit) == ((col >> bit) ^ 1)
        halves = [split(x) for x in inverses]
        right = [split(dot3(n, x)) for n, x in zip(lowers, halves)]
        whole = [dot3(x, y) for x, y in zip(halves, right)]
        inverses = [x - jnp.where(mask, w, 0.0) for x, w in zip(inverses, whole)]
        bit += 1
    return inverses


def group_terms(group):
    rows, width = group[0][1].shape
    wide_v = group[0][2].shape[1]
    half = rows // 2
    row, col = iotas(rows)
    lane = lax.broadcasted_iota(jnp.int32, (rows, 128), 1)
    lowers, sides, blocks = [], [], []
    for q, k, v, beta in group:
        rk = inverse_unit_norm(k.astype(F32))
        packed = jnp.where(lane == 0, rk, jnp.where(lane == 1, beta, 0.0)).T
        lower = jnp.where(row > col, dot(k, k, NT) * (beta * rk) * packed[0:1], 0.0)
        lowers.append(lower)
        sides.append((rk, packed[0:1], packed[1:2]))
        blocks += [lower[:half, :half], lower[half:, half:]]
    diagonal = unit_lower_inverses(blocks)
    halves = [split(x) for x in diagonal]
    corners = [
        split(dot3(split(n[half:, :half]), halves[2 * i])) for i, n in enumerate(lowers)
    ]
    corners = [dot3(halves[2 * i + 1], c) for i, c in enumerate(corners)]
    zero = jnp.zeros((half, half), F32)
    inverses = [
        jnp.concatenate(
            [
                jnp.concatenate([diagonal[2 * i], zero], axis=1),
                jnp.concatenate([-c, diagonal[2 * i + 1]], axis=1),
            ],
            axis=0,
        )
        for i, c in enumerate(corners)
    ]
    eye = jnp.where(iotas(width)[0] == iotas(width)[1], 1.0, 0.0)
    results = []
    for (q, k, v, beta), (rk, rk_row, beta_row), inv in zip(group, sides, inverses):
        inv_v = inv * beta_row
        ubar = dot2(split(inv_v), v)
        wmat = dot2(split(inv_v * rk_row), k)
        both = jnp.concatenate([ubar, wmat], axis=1)
        maps = dot2(split(both * rk), k, TN)
        results.append((eye - maps[wide_v:], maps[:wide_v], both, rk_row))
    return results


def query_terms(q, k, both, rk_row):
    rows = q.shape[0]
    wide_v = both.shape[1] - k.shape[1]
    row, col = iotas(rows)
    qf = q.astype(F32)
    rq = inverse_unit_norm(qf)
    scores = jnp.where(row >= col, dot(q, k, NT) * rq * rk_row, 0.0)
    mixed = dot3(split(scores), split(both))
    return mixed[:, :wide_v], qf * rq - mixed[:, wide_v:]


def maps_kernel(
    segs, inners, q_ref, k_ref, v_ref, s_ref, out_ref, in_ref, lo_ref, qh_ref, ql_ref,
    wide, qs, ks, vs, solved, scale, own, earlier, pair_h, pair_l, pair_o, landed, leaving,
    staged, map_send, map_recv, next_send, fan_send, state_recv, load_sem,
):
    heads = q_ref.shape[1]
    wide_k = own.shape[2]
    total = segs * inners
    me = lax.axis_index("seg") * inners + lax.axis_index("inner")
    odd = lax.rem(me, 2) == 1
    even = lax.rem(me, 2) == 0
    first = me < 2
    last = me >= total - 2

    def place(index):
        index = lax.rem(index + total, total)
        return {"seg": index // inners, "inner": lax.rem(index, inners)}

    barrier = pltpu.get_barrier_semaphore()
    for step in (-2, -1, 1, 2):
        pl.semaphore_signal(barrier, inc=1, device_id=place(me + step), device_id_type=pl.DeviceIdType.MESH)

    def send(source, target, send_sem, recv_sem, h, step):
        return pltpu.make_async_remote_copy(
            src_ref=source.at[h],
            dst_ref=target.at[h],
            send_sem=send_sem.at[h],
            recv_sem=recv_sem.at[h],
            device_id=place(me + step),
            device_id_type=pl.DeviceIdType.MESH,
        )

    def map_hop(h):
        return send(own, earlier, map_send, map_recv, h, 1)

    def next_hop(h):
        return send(leaving, landed, next_send, state_recv, h, 2)

    def fan_hop(h):
        return send(landed, landed, fan_send, state_recv, h, -1)

    loads = [
        pltpu.make_async_copy(source, staged.at[i], load_sem.at[i])
        for i, source in enumerate((k_ref, v_ref, q_ref))
    ]
    for load in loads:
        load.start()
    for i, target in enumerate((ks, vs, qs)):
        loads[i].wait()
        wide[...] = staged[i].astype(F32)
        for h in range(heads):
            target[h] = wide[:, h, :].astype(BF16)
    strengths = s_ref[...]
    lane = lax.broadcasted_iota(jnp.int32, strengths.shape, 1)
    pl.semaphore_wait(barrier, 4)

    def local(step, unused):
        places = [step * GROUP + i for i in range(GROUP)]
        group = []
        for h in places:
            beta = jnp.sum(jnp.where(lane == h, strengths, 0.0), axis=1, keepdims=True)
            group.append((qs[h], ks[h], vs[h], beta))
        terms = group_terms(group)
        for h, (trans, offset, both, rk_row) in zip(places, terms):
            own[h, :wide_k, :] = trans
            own[h, wide_k:, :] = offset
            solved[h] = both
            scale[h] = jnp.broadcast_to(rk_row, scale.shape[1:])

        @pl.when(jnp.logical_and(even, jnp.logical_or(me < total // 2, step < heads // GROUP - 1)))
        def _():
            for h in places:
                map_hop(h).start()

        return unused

    lax.fori_loop(0, heads // GROUP, local, 0)

    def query_side(step, unused):
        for i in range(GROUP):
            h = step * GROUP + i
            lo_ref[h], fix = query_terms(qs[h], ks[h], solved[h], scale[h, 0:1, :])
            qh_ref[h], ql_ref[h] = split(fix)
        return unused

    early = jnp.logical_and(odd, me < total // 2)

    @pl.when(jnp.logical_not(early))
    def _():
        lax.fori_loop(0, heads // GROUP, query_side, 0)

    @pl.when(jnp.logical_and(even, me >= total // 2))
    def _():
        for h in range(heads - GROUP, heads):
            map_hop(h).start()

    def enter(h):
        in_ref[h] = dot3(split(landed[h]), split(earlier[h, :wide_k, :])) + earlier[h, wide_k:, :]

    @pl.when(odd)
    def _():
        def compose(h):
            map_hop(h).wait_recv()
            later = split(own[h, :wide_k, :])

            @pl.when(first)
            def _():
                offset = dot3(split(earlier[h, wide_k:, :]), later)
                leaving[h] = offset + own[h, wide_k:, :]
                next_hop(h).start()

            @pl.when(jnp.logical_not(first))
            def _():
                both = dot3(split(earlier[h]), later)
                pair_h[h], pair_l[h] = split(both[:wide_k])
                pair_o[h] = both[wide_k:] + own[h, wide_k:, :]

        def advance(h, unused):
            next_hop(h).wait_recv()

            @pl.when(jnp.logical_not(last))
            def _():
                leaving[h] = dot3(split(landed[h]), (pair_h[h], pair_l[h])) + pair_o[h]
                next_hop(h).start()

            fan_hop(h).start()

            @pl.when(last)
            def _():
                enter(h)

            return unused

        for low, high in ((0, heads - GROUP), (heads - GROUP, heads)):
            for h in range(low, high):
                compose(h)

            @pl.when(jnp.logical_not(first))
            def _():
                lax.fori_loop(low, high, advance, 0)

        @pl.when(first)
        def _():
            for h in range(heads):
                in_ref[h] = earlier[h, wide_k:, :]

        @pl.when(jnp.logical_not(jnp.logical_or(first, last)))
        def _():
            for h in range(heads):
                enter(h)

    @pl.when(early)
    def _():
        lax.fori_loop(0, heads // GROUP, query_side, 0)

    @pl.when(jnp.logical_and(odd, jnp.logical_not(last)))
    def _():
        for h in range(heads):
            next_hop(h).wait_send()

    @pl.when(jnp.logical_and(odd, jnp.logical_not(first)))
    def _():
        for h in range(heads):
            fan_hop(h).wait_send()

    @pl.when(even)
    def _():
        for h in range(heads):
            map_hop(h).wait_send()

        @pl.when(first)
        def _():
            in_ref[...] = jnp.zeros_like(in_ref)

        @pl.when(jnp.logical_not(first))
        def _():
            for h in range(heads):
                fan_hop(h).wait_recv()
            in_ref[...] = landed[...]

    emit_kernel(in_ref, lo_ref, qh_ref, ql_ref, out_ref, wide)


def emit_kernel(in_ref, lo_ref, qh_ref, ql_ref, out_ref, wide):
    heads = in_ref.shape[0]
    for h in range(heads):
        wide[:, h, :] = lo_ref[h] + dot3((qh_ref[h], ql_ref[h]), split(in_ref[h]), NT)
    out_ref[...] = wide[...].astype(out_ref.dtype)


def body(segs, inners, queries, keys, values, strengths):
    rows, heads, width = queries.shape
    wide_v = values.shape[2]
    vm = pl.BlockSpec(memory_space=pltpu.VMEM)
    shape = jax.ShapeDtypeStruct
    dma = pltpu.SemaphoreType.DMA((heads,))
    maps = pltpu.VMEM((heads, width + wide_v, width), F32)
    halves = pltpu.VMEM((heads, width, width), BF16)
    states = pltpu.VMEM((heads, wide_v, width), F32)
    return pl.pallas_call(
        functools.partial(maps_kernel, segs, inners),
        out_shape=shape((rows, heads, wide_v), BF16),
        in_specs=[pl.BlockSpec(memory_space=pltpu.HBM)] * 3 + [vm],
        out_specs=vm,
        scratch_shapes=[
            states,
            pltpu.VMEM((heads, rows, wide_v), F32),
            pltpu.VMEM((heads, rows, width), BF16),
            pltpu.VMEM((heads, rows, width), BF16),
            pltpu.VMEM((rows, heads, width), F32),
            pltpu.VMEM((heads, rows, width), BF16),
            pltpu.VMEM((heads, rows, width), BF16),
            pltpu.VMEM((heads, rows, wide_v), BF16),
            pltpu.VMEM((heads, rows, wide_v + width), F32),
            pltpu.VMEM((heads, 8, rows), F32),
            maps, maps, halves, halves, states, states, states,
            pltpu.VMEM((3, rows, heads, width), BF16),
            dma, dma, dma, dma, dma,
            pltpu.SemaphoreType.DMA((3,)),
        ],
        compiler_params=pltpu.CompilerParams(
            collective_id=0, has_side_effects=True, vmem_limit_bytes=60 * 1024 * 1024
        ),
        name="maps_and_chain",
    )(queries, keys, values, strengths)


def solution(mesh):
    split_rows = ("grp", "seg", "inner")
    placed = (
        P(split_rows, None, None),
        P(split_rows, None, None),
        P(split_rows, None, None),
        P(split_rows, None),
    )
    return jax.shard_map(
        functools.partial(body, mesh.shape["seg"], mesh.shape["inner"]),
        mesh=mesh,
        in_specs=placed,
        out_specs=P(split_rows, None, None),
        check_vma=False,
    )
```
